32 devices in a mesh: task: 4 (over z), unit: 8 (over y, x, core).
Axes of the slice: x: 2, y: 2, z: 4, core: 2. Of those that a mesh axis runs over, the one named last changes fastest.
Arguments:
- tokens: bfloat16 [64, 4096], P(('task', 'unit')), may hold values from -6 to 6
- router: float32 [64, 4], P('unit', 'task'), may hold values from 0.1 to 1
- base_gate: bfloat16 [16384, 4096], P(('task', 'unit')), may hold values from -0.09375 to 0.09375
- base_up: bfloat16 [16384, 4096], P(('task', 'unit')), may hold values from -0.09375 to 0.09375
- base_down: bfloat16 [16384, 4096], P(('task', 'unit')), may hold values from -0.046875 to 0.046875
- task_gate: bfloat16 [4, 16384, 4096], P('task', 'unit'), may hold values from -0.09375 to 0.09375
- task_up: bfloat16 [4, 16384, 4096], P('task', 'unit'), may hold values from -0.09375 to 0.09375
- task_down: bfloat16 [4, 16384, 4096], P('task', 'unit'), may hold values from -0.046875 to 0.046875
Outputs:
- mixed: bfloat16 [64, 4096], P(('task', 'unit'))
The draws below stay inside these ranges and needn't reach their ends.
All inputs are finite; a program needn't handle non-finite values.
Results may differ from the reference program's by a relative error of at most 0.0049.
Values may be sent and summed in bfloat16 or wider, within the bound.
A program may use at most 128 MiB of HBM per device.

```python
import jax
import jax.numpy as jnp

D = 4096
FF = 16384
KTASK = 4
TOKENS = 64


def shard_levels(rng, shape, pieces, smallest, top_value):
    loudness, own = 1.0, jax.random.fold_in(rng, 6)
    for dim, parts in pieces:
        steps = jnp.exp(jax.random.uniform(jax.random.fold_in(own, dim), (parts,), jnp.float32, smallest / len(pieces), top_value / len(pieces)))
        loudness = loudness * jnp.repeat(steps, shape[dim] // parts).reshape([-1 if axis == dim else 1 for axis in range(len(shape))])
    return loudness


def scatter_about(own_key, extent, scale, limit, cuts=(), kind=jnp.bfloat16):
    entries = scale * jax.random.normal(own_key, extent, jnp.float32)
    if cuts:
        entries = entries * shard_levels(own_key, extent, cuts, -0.22, 0.18)
    return jnp.clip(entries, -limit, limit).astype(kind)


def setup_inputs(seed: int = 0) -> dict:
    key_of = jax.random.split(jax.random.key(seed), 9)
    return {
        "tokens": scatter_about(key_of[0], (TOKENS, D), 1.0, 6.0, ((0, 32),)),
        "router": jnp.clip(0.1 + 0.9 * jax.random.uniform(key_of[1], (TOKENS, KTASK), jnp.float32) ** shard_levels(key_of[1], (TOKENS, KTASK), ((0, 8), (1, 4)), -0.2, 0.2), 0.1, 1.0),
        "base_gate": scatter_about(key_of[2], (FF, D), D ** -0.5, 0.09375, ((0, 32),)),
        "base_up": scatter_about(key_of[3], (FF, D), D ** -0.5, 0.09375, ((0, 32),)),
        "base_down": scatter_about(key_of[4], (FF, D), FF ** -0.5, 0.046875, ((0, 32),)),
        "task_gate": scatter_about(key_of[5], (KTASK, FF, D), D ** -0.5, 0.09375, ((0, 4), (1, 8))),
        "task_up": scatter_about(key_of[6], (KTASK, FF, D), D ** -0.5, 0.09375, ((0, 4), (1, 8))),
        "task_down": scatter_about(key_of[7], (KTASK, FF, D), FF ** -0.5, 0.046875, ((0, 4), (1, 8))),
    }


def swiglu(rows, gate, upper):
    gated = jnp.dot(rows, gate.T, preferred_element_type=jnp.float32)
    lifted = jnp.dot(rows, upper.T, preferred_element_type=jnp.float32)
    return jax.nn.silu(gated) * lifted


def reference(tokens, router, base_gate, base_up, base_down, task_gate, task_up, task_down):
    base_hidden = swiglu(tokens, base_gate, base_up).astype(jnp.bfloat16)
    total = jnp.dot(base_hidden, base_down, preferred_element_type=jnp.float32)
    for index in range(KTASK):
        scaled = swiglu(tokens, task_gate[index], task_up[index]) * router[:, index:index + 1]
        task_hidden = scaled.astype(jnp.bfloat16)
        total = total + jnp.dot(task_hidden, task_down[index], preferred_element_type=jnp.float32)
    return total.astype(jnp.bfloat16)
```

```python
import functools
import math

import jax
import jax.numpy as jnp
from jax import lax
from jax.experimental import pallas as pl
from jax.experimental.pallas import tpu as pltpu
from jax.sharding import PartitionSpec as P

MESH = pl.DeviceIdType.MESH
F32 = jnp.float32
BF16 = jnp.bfloat16
COLS = 512
REUSE = 1


def kernel(
    n_task, n_unit, tok_ref, router_ref, bg, bu, bd, tg, tu, td, out_ref,
    gate_v, up_v, down_v, hid, x_v, tokbuf, g1, rows8, wbuf, wcol,
    part, send_a, recv_a, send_b, recv_b, send_c, recv_c, own_c,
    gsem, usem, dsem, g1s, g1r, g2s, g2r, g3s, g3r, ws, wr,
    as_, ar, bs, br, cs, cr,
):
    t = lax.axis_index("task")
    u = lax.axis_index("unit")
    n_xy = n_unit // 2
    c = lax.rem(u, 2)
    xy = u // 2
    rows, d_model = tok_ref.shape
    group = n_task * rows
    tokens = group * n_unit
    half = tokens // 2
    base_w, task_w = bg.shape[0], tg.shape[1]
    n_hid, _, unit_w = hid.shape
    n_base = base_w // unit_w
    n_col = d_model // COLS
    kept = n_col - REUSE

    for i in range(n_hid):
        for base, task, buf, sem in ((bg, tg, gate_v, gsem), (bu, tu, up_v, usem)):
            if i < n_base:
                src = base.at[pl.ds(i * unit_w, unit_w)]
            else:
                src = task.at[0, pl.ds((i - n_base) * unit_w, unit_w)]
            pltpu.make_async_copy(src, buf.at[pl.ds(i * unit_w, unit_w)], sem.at[i]).start()

    def down_copies(j):
        cols = pl.ds(j * COLS, COLS)
        if j < kept:
            lo, hi = down_v.at[j, pl.ds(0, base_w)], down_v.at[j, pl.ds(base_w, task_w)]
        else:
            spot = pl.ds((j - kept) * COLS, COLS)
            lo, hi = gate_v.at[pl.ds(0, base_w), spot], gate_v.at[pl.ds(base_w, task_w), spot]
        return (
            pltpu.make_async_copy(bd.at[:, cols], lo, dsem.at[j, 0]),
            pltpu.make_async_copy(td.at[0, :, cols], hi, dsem.at[j, 1]),
        )

    for j in range(kept):
        for copy in down_copies(j):
            copy.start()

    barrier = pltpu.get_barrier_semaphore()
    for d in range(1, n_task):
        pl.semaphore_signal(barrier, inc=1, device_id=(lax.rem(t + d, n_task), u), device_id_type=MESH)
    for d in range(1, n_unit):
        pl.semaphore_signal(barrier, inc=1, device_id=(t, lax.rem(u + d, n_unit)), device_id_type=MESH)
    pl.semaphore_wait(barrier, n_task + n_unit - 2)

    def remote(src, dst, ssem, rsem, dev):
        return pltpu.make_async_remote_copy(
            src_ref=src, dst_ref=dst, send_sem=ssem, recv_sem=rsem, device_id=dev, device_id_type=MESH
        )

    sibling = (t, xy * 2 + 1 - c)

    def peer_xy(d):
        return lax.rem(xy + d, n_xy)

    first = [
        remote(tok_ref, g1.at[t], g1s.at[d], g1r.at[d], (lax.rem(t + d, n_task), u))
        for d in range(1, n_task)
    ]
    for copy in first:
        copy.start()
    weights = [
        remote(router_ref, wbuf.at[u], ws.at[d], wr.at[d], (t, lax.rem(u + d, n_unit)))
        for d in range(1, n_unit)
    ]
    for copy in weights:
        copy.start()
    g1[t] = tok_ref[...]
    wbuf[u] = router_ref[...]
    for copy in first:
        copy.wait()
    for s in range(n_task):
        rows8[pl.ds(s * rows, rows), :] = g1[s].astype(F32)
    whole = rows8[...]
    mid = d_model // 2
    tokbuf[c, xy] = jnp.concatenate([whole[:, :mid], whole[:, mid:]], 0).astype(BF16)
    second = [
        remote(tokbuf.at[c, xy], tokbuf.at[c, xy], g2s.at[d], g2r.at[d], (t, peer_xy(d) * 2 + c))
        for d in range(1, n_xy)
    ]
    for copy in second:
        copy.start()
    third = [remote(tokbuf.at[c, xy], tokbuf.at[c, xy], g3s.at[0], g3r.at[0], sibling)]
    third[0].start()
    for d in range(1, n_xy):
        came = lax.rem(xy + n_xy - d, n_xy)
        remote(tokbuf.at[c, came], tokbuf.at[c, came], g2s.at[d], g2r.at[d], sibling).wait_recv()
        third.append(remote(tokbuf.at[c, came], tokbuf.at[c, came], g3s.at[d], g3r.at[d], sibling))
        third[-1].start()

    for copy in weights:
        copy.wait()
    shape = (tokens, group)
    place = lax.broadcasted_iota(jnp.int32, shape, 0)
    lane = lax.broadcasted_iota(jnp.int32, shape, 1)
    block = place // group
    unit_of = lax.rem(block, n_xy) * 2 + block // n_xy
    inner = lax.rem(place, group)
    token = ((inner // rows) * n_unit + unit_of) * rows + lax.rem(inner, rows)
    picked = jnp.zeros(shape, F32)
    for s in range(n_unit):
        picked = picked + jnp.where(token == lane + s * group, wbuf[s], 0.0)
    wcol[...] = jnp.broadcast_to(jnp.sum(picked, 1, keepdims=True), wcol.shape)

    for copy in second:
        copy.wait_send()
    for copy in third:
        copy.wait()
    for core in range(2):
        for p in range(0, n_xy, 2):
            parts = []
            for q in (p, p + 1):
                both = tokbuf[core, q].astype(F32)
                parts.append(jnp.concatenate([both[:group], both[group:]], 1))
            x_v[pl.ds((core * n_xy + p) * group, 2 * group), :] = jnp.concatenate(parts, 0).astype(BF16)

    dims = (((1,), (1,)), ((), ()))

    def hidden(i, _):
        spot = pl.ds(pl.multiple_of(i * unit_w, unit_w), unit_w)
        pltpu.make_async_copy(tg.at[0, pl.ds(0, unit_w)], gate_v.at[spot], gsem.at[i]).wait()
        pltpu.make_async_copy(tu.at[0, pl.ds(0, unit_w)], up_v.at[spot], usem.at[i]).wait()
        x = x_v[...]
        g = lax.dot_general(x, gate_v[spot, :], dims, preferred_element_type=F32)
        v = lax.dot_general(x, up_v[spot, :], dims, preferred_element_type=F32)
        scale = jnp.where(i < n_base, 1.0, wcol[:, :1])
        hid[i] = (jax.nn.silu(g) * v * scale).astype(BF16)
        return 0

    lax.fori_loop(0, n_hid, hidden, 0)

    for j in range(kept, n_col):
        for copy in down_copies(j):
            copy.start()

    pending = []

    def stage_a(j):
        for copy in down_copies(j):
            copy.wait()
        weight = down_v.at[j] if j < kept else gate_v.at[:, pl.ds((j - kept) * COLS, COLS)]
        if unit_w % 128 == 0:
            h = jnp.concatenate([hid[i] for i in range(n_hid)], 1)
            total = jnp.dot(h, weight[...], preferred_element_type=F32)
        else:
            total = jnp.zeros((tokens, COLS), F32)
            for i in range(n_hid):
                total += jnp.dot(hid[i], weight[pl.ds(i * unit_w, unit_w), :], preferred_element_type=F32)
        part[j] = total.reshape(2, n_xy, group, COLS)
        send_a[j] = part[j, 1 - c].reshape(half, COLS).astype(BF16)
        copy = remote(send_a.at[j], recv_a.at[j], as_.at[j], ar.at[j], sibling)
        copy.start()
        pending.append(copy)

    def stage_b(j):
        remote(send_a.at[j], recv_a.at[j], as_.at[j], ar.at[j], sibling).wait_recv()
        part[j, c] += recv_a[j].astype(F32).reshape(n_xy, group, COLS)
        for d in range(1, n_xy):
            block = part[j, c, peer_xy(d)]
            send_b[j, d] = jnp.concatenate([block[:, : COLS // 2], block[:, COLS // 2 :]], 0).astype(BF16)
            copy = remote(send_b.at[j, d], recv_b.at[j, d], bs.at[j, d], br.at[j, d], (t, peer_xy(d) * 2 + c))
            copy.start()
            pending.append(copy)

    def stage_c(j):
        total = part[j, c, xy]
        for d in range(1, n_xy):
            remote(send_b.at[j, d], recv_b.at[j, d], bs.at[j, d], br.at[j, d], sibling).wait_recv()
            both = recv_b[j, d].astype(F32)
            total = total + jnp.concatenate([both[:group], both[group:]], 1)
        for s in range(n_task):
            piece = total[s * rows : (s + 1) * rows]
            own_c[j, s] = piece
            send_c[j, s] = piece.astype(BF16)
        for d in range(1, n_task):
            to = lax.rem(t + d, n_task)
            copy = remote(send_c.at[j, to], recv_c.at[j, d], cs.at[j, d], cr.at[j, d], (to, u))
            copy.start()
            pending.append(copy)

    def stage_d(j):
        total = own_c[j, t]
        for d in range(1, n_task):
            remote(send_c.at[j, 0], recv_c.at[j, d], cs.at[j, d], cr.at[j, d], sibling).wait_recv()
            total = total + recv_c[j, d].astype(F32)
        out_ref[:, pl.ds(j * COLS, COLS)] = total.astype(BF16)

    for step in range(n_col + 3):
        for lag, stage in enumerate((stage_a, stage_b, stage_c, stage_d)):
            if 0 <= step - lag < n_col:
                stage(step - lag)
    for copy in pending:
        copy.wait_send()


def body(n_task, n_unit, tokens, router, bg, bu, bd, tg, tu, td):
    rows, d_model = tokens.shape
    group = n_task * rows
    total = group * n_unit
    n_xy = n_unit // 2
    base_w, task_w = bg.shape[0], tg.shape[1]
    unit_w = min(256, math.gcd(base_w, task_w))
    width = base_w + task_w
    n_hid = width // unit_w
    n_col = d_model // COLS
    half = total // 2
    vmem = pl.BlockSpec(memory_space=pltpu.VMEM)
    hbm = pl.BlockSpec(memory_space=pl.ANY)
    dma = pltpu.SemaphoreType.DMA
    return pl.pallas_call(
        functools.partial(kernel, n_task, n_unit),
        out_shape=jax.ShapeDtypeStruct((rows, d_model), BF16),
        in_specs=[vmem, vmem] + [hbm] * 6,
        out_specs=vmem,
        scratch_shapes=[
            pltpu.VMEM((width, d_model), BF16),
            pltpu.VMEM((width, d_model), BF16),
            pltpu.VMEM((n_col - REUSE, width, COLS), BF16),
            pltpu.VMEM((n_hid, total, unit_w), BF16),
            pltpu.VMEM((total, d_model), BF16),
            pltpu.VMEM((2, n_xy, 2 * group, d_model // 2), BF16),
            pltpu.VMEM((n_task, rows, d_model), BF16),
            pltpu.VMEM((group, d_model), F32),
            pltpu.VMEM((n_unit, 1, group), F32),
            pltpu.VMEM((total, 128), F32),
            pltpu.VMEM((n_col, 2, n_xy, group, COLS), F32),
            pltpu.VMEM((n_col, half, COLS), BF16),
            pltpu.VMEM((n_col, half, COLS), BF16),
            pltpu.VMEM((n_col, n_xy, 2 * group, COLS // 2), BF16),
            pltpu.VMEM((n_col, n_xy, 2 * group, COLS // 2), BF16),
            pltpu.VMEM((n_col, n_task, rows, COLS), BF16),
            pltpu.VMEM((n_col, n_task, rows, COLS), BF16),
            pltpu.VMEM((n_col, n_task, rows, COLS), F32),
            dma((n_hid,)), dma((n_hid,)), dma((n_col, 2)),
            dma((n_task,)), dma((n_task,)),
            dma((n_xy,)), dma((n_xy,)), dma((n_xy,)), dma((n_xy,)),
            dma((n_unit,)), dma((n_unit,)),
            dma((n_col,)), dma((n_col,)),
            dma((n_col, n_xy)), dma((n_col, n_xy)),
            dma((n_col, n_task)), dma((n_col, n_task)),
        ],
        compiler_params=pltpu.CompilerParams(
            collective_id=0, has_side_effects=True, vmem_limit_bytes=VMEM_LIMIT
        ),
        cost_estimate=pl.CostEstimate(
            flops=6 * total * width * d_model,
            bytes_accessed=6 * width * d_model,
            transcendentals=total * width,
        ),
        name="router_mixture",
    )(tokens, router.reshape(1, group), bg, bu, bd, tg, tu, td)


VMEM_LIMIT = 64 * 1024 * 1024


def solution(mesh):
    in_specs = (
        P(("task", "unit"), None),
        P("unit", "task"),
        P(("task", "unit"), None),
        P(("task", "unit"), None),
        P(("task", "unit"), None),
        P("task", "unit", None),
        P("task", "unit", None),
        P("task", "unit", None),
    )
    out_specs = P(("task", "unit"), None)
    part_fn = functools.partial(body, mesh.shape["task"], mesh.shape["unit"])
    return jax.shard_map(part_fn, mesh=mesh, in_specs=in_specs, out_specs=out_specs, check_vma=False)
```

```python
import functools
import math

import jax
import jax.numpy as jnp
from jax import lax
from jax.experimental import pallas as pl
from jax.experimental.pallas import tpu as pltpu
from jax.sharding import PartitionSpec as P

MESH = pl.DeviceIdType.MESH
F32 = jnp.float32
BF16 = jnp.bfloat16
COLS = 1024
LAG = 4
REUSE = 1


def kernel(
    n_task, n_unit, tok_ref, router_ref, bg, bu, bd, tg, tu, td, out_ref,
    gate_v, up_v, down_v, hid, x_v, tokbuf, g1, rows8, wbuf, wcol,
    part, send_a, recv_a, send_b, recv_b, send_c, recv_c, own_c,
    gsem, usem, dsem, g1s, g1r, g2s, g2r, g3s, g3r, ws, wr,
    as_, ar, bs, br, cs, cr,
):
    t = lax.axis_index("task")
    u = lax.axis_index("unit")
    n_xy = n_unit // 2
    c = lax.rem(u, 2)
    xy = u // 2
    rows, d_model = tok_ref.shape
    group = n_task * rows
    tokens = group * n_unit
    half = tokens // 2
    base_w, task_w = bg.shape[0], tg.shape[1]
    n_hid, _, unit_w = hid.shape
    n_base = base_w // unit_w
    n_col = d_model // COLS
    kept = n_col - REUSE

    for i in range(n_hid):
        for base, task, buf, sem in ((bg, tg, gate_v, gsem), (bu, tu, up_v, usem)):
            if i < n_base:
                src = base.at[pl.ds(i * unit_w, unit_w)]
            else:
                src = task.at[0, pl.ds((i - n_base) * unit_w, unit_w)]
            pltpu.make_async_copy(src, buf.at[pl.ds(i * unit_w, unit_w)], sem.at[i]).start()

    def down_copies(j):
        cols = pl.ds(j * COLS, COLS)
        if j < kept:
            lo, hi = down_v.at[j, pl.ds(0, base_w)], down_v.at[j, pl.ds(base_w, task_w)]
        else:
            spot = pl.ds((j - kept) * COLS, COLS)
            lo, hi = gate_v.at[pl.ds(0, base_w), spot], gate_v.at[pl.ds(base_w, task_w), spot]
        return (
            pltpu.make_async_copy(bd.at[:, cols], lo, dsem.at[j, 0]),
            pltpu.make_async_copy(td.at[0, :, cols], hi, dsem.at[j, 1]),
        )

    for j in range(kept):
        for copy in down_copies(j):
            copy.start()

    barrier = pltpu.get_barrier_semaphore()
    for d in range(1, n_task):
        pl.semaphore_signal(barrier, inc=1, device_id=(lax.rem(t + d, n_task), u), device_id_type=MESH)
    for d in range(1, n_unit):
        pl.semaphore_signal(barrier, inc=1, device_id=(t, lax.rem(u + d, n_unit)), device_id_type=MESH)
    pl.semaphore_wait(barrier, n_task + n_unit - 2)

    def remote(src, dst, ssem, rsem, dev):
        return pltpu.make_async_remote_copy(
            src_ref=src, dst_ref=dst, send_sem=ssem, recv_sem=rsem, device_id=dev, device_id_type=MESH
        )

    sibling = (t, xy * 2 + 1 - c)

    def peer_xy(d):
        return lax.rem(xy + d, n_xy)

    first = [
        remote(tok_ref, g1.at[t], g1s.at[d], g1r.at[d], (lax.rem(t + d, n_task), u))
        for d in range(1, n_task)
    ]
    for copy in first:
        copy.start()
    weights = [
        remote(router_ref, wbuf.at[u], ws.at[d], wr.at[d], (t, lax.rem(u + d, n_unit)))
        for d in range(1, n_unit)
    ]
    for copy in weights:
        copy.start()
    g1[t] = tok_ref[...]
    wbuf[u] = router_ref[...]
    for copy in first:
        copy.wait()
    for s in range(n_task):
        rows8[pl.ds(s * rows, rows), :] = g1[s].astype(F32)
    whole = rows8[...]
    mid = d_model // 2
    tokbuf[c, xy] = jnp.concatenate([whole[:, :mid], whole[:, mid:]], 0).astype(BF16)
    second = [
        remote(tokbuf.at[c, xy], tokbuf.at[c, xy], g2s.at[d], g2r.at[d], (t, peer_xy(d) * 2 + c))
        for d in range(1, n_xy)
    ]
    for copy in second:
        copy.start()
    third = [remote(tokbuf.at[c, xy], tokbuf.at[c, xy], g3s.at[0], g3r.at[0], sibling)]
    third[0].start()
    for d in range(1, n_xy):
        came = lax.rem(xy + n_xy - d, n_xy)
        remote(tokbuf.at[c, came], tokbuf.at[c, came], g2s.at[d], g2r.at[d], sibling).wait_recv()
        third.append(remote(tokbuf.at[c, came], tokbuf.at[c, came], g3s.at[d], g3r.at[d], sibling))
        third[-1].start()

    for copy in weights:
        copy.wait()
    shape = (tokens, group)
    place = lax.broadcasted_iota(jnp.int32, shape, 0)
    lane = lax.broadcasted_iota(jnp.int32, shape, 1)
    block = place // group
    unit_of = lax.rem(block, n_xy) * 2 + block // n_xy
    inner = lax.rem(place, group)
    token = ((inner // rows) * n_unit + unit_of) * rows + lax.rem(inner, rows)
    picked = jnp.zeros(shape, F32)
    for s in range(n_unit):
        picked = picked + jnp.where(token == lane + s * group, wbuf[s], 0.0)
    wcol[...] = jnp.broadcast_to(jnp.sum(picked, 1, keepdims=True), wcol.shape)

    for copy in second:
        copy.wait_send()
    for copy in third:
        copy.wait()
    for core in range(2):
        for p in range(0, n_xy, 2):
            parts = []
            for q in (p, p + 1):
                both = tokbuf[core, q].astype(F32)
                parts.append(jnp.concatenate([both[:group], both[group:]], 1))
            x_v[pl.ds((core * n_xy + p) * group, 2 * group), :] = jnp.concatenate(parts, 0).astype(BF16)

    dims = (((1,), (1,)), ((), ()))

    def hidden(i, _):
        spot = pl.ds(pl.multiple_of(i * unit_w, unit_w), unit_w)
        pltpu.make_async_copy(tg.at[0, pl.ds(0, unit_w)], gate_v.at[spot], gsem.at[i]).wait()
        pltpu.make_async_copy(tu.at[0, pl.ds(0, unit_w)], up_v.at[spot], usem.at[i]).wait()
        x = x_v[...]
        g = lax.dot_general(x, gate_v[spot, :], dims, preferred_element_type=F32)
        v = lax.dot_general(x, up_v[spot, :], dims, preferred_element_type=F32)
        scale = jnp.where(i < n_base, 1.0, wcol[:, :1])
        hid[i] = (jax.nn.silu(g) * v * scale).astype(BF16)
        return 0

    lax.fori_loop(0, n_hid, hidden, 0)

    for j in range(kept, n_col):
        for copy in down_copies(j):
            copy.start()

    pending = []

    def stage_a(j):
        for copy in down_copies(j):
            copy.wait()
        weight = down_v.at[j] if j < kept else gate_v.at[:, pl.ds((j - kept) * COLS, COLS)]
        if unit_w % 128 == 0:
            h = jnp.concatenate([hid[i] for i in range(n_hid)], 1)
            total = jnp.dot(h, weight[...], preferred_element_type=F32)
        else:
            total = jnp.zeros((tokens, COLS), F32)
            for i in range(n_hid):
                total += jnp.dot(hid[i], weight[pl.ds(i * unit_w, unit_w), :], preferred_element_type=F32)
        part[j] = total.reshape(2, n_xy, group, COLS)
        send_a[j] = part[j, 1 - c].reshape(half, COLS).astype(BF16)
        copy = remote(send_a.at[j], recv_a.at[j], as_.at[j], ar.at[j], sibling)
        copy.start()
        pending.append(copy)

    def stage_b(j):
        remote(send_a.at[j], recv_a.at[j], as_.at[j], ar.at[j], sibling).wait_recv()
        part[j, c] += recv_a[j].astype(F32).reshape(n_xy, group, COLS)
        for d in range(1, n_xy):
            block = part[j, c, peer_xy(d)]
            send_b[j, d] = jnp.concatenate([block[:, : COLS // 2], block[:, COLS // 2 :]], 0).astype(BF16)
            copy = remote(send_b.at[j, d], recv_b.at[j, d], bs.at[j, d], br.at[j, d], (t, peer_xy(d) * 2 + c))
            copy.start()
            pending.append(copy)

    def stage_c(j):
        total = part[j, c, xy]
        for d in range(1, n_xy):
            remote(send_b.at[j, d], recv_b.at[j, d], bs.at[j, d], br.at[j, d], sibling).wait_recv()
            both = recv_b[j, d].astype(F32)
            total = total + jnp.concatenate([both[:group], both[group:]], 1)
        for s in range(n_task):
            piece = total[s * rows : (s + 1) * rows]
            own_c[j, s] = piece
            send_c[j, s] = piece.astype(BF16)
        for d in range(1, n_task):
            to = lax.rem(t + d, n_task)
            copy = remote(send_c.at[j, to], recv_c.at[j, d], cs.at[j, d], cr.at[j, d], (to, u))
            copy.start()
            pending.append(copy)

    def stage_d(j):
        total = own_c[j, t]
        for d in range(1, n_task):
            remote(send_c.at[j, 0], recv_c.at[j, d], cs.at[j, d], cr.at[j, d], sibling).wait_recv()
            total = total + recv_c[j, d].astype(F32)
        out_ref[:, pl.ds(j * COLS, COLS)] = total.astype(BF16)

    for step in range(n_col + 3 * LAG):
        for lag, stage in ((0, stage_a), (LAG, stage_b), (2 * LAG, stage_c), (3 * LAG, stage_d)):
            if 0 <= step - lag < n_col:
                stage(step - lag)
    for copy in pending:
        copy.wait_send()


def body(n_task, n_unit, tokens, router, bg, bu, bd, tg, tu, td):
    rows, d_model = tokens.shape
    group = n_task * rows
    total = group * n_unit
    n_xy = n_unit // 2
    base_w, task_w = bg.shape[0], tg.shape[1]
    unit_w = min(512, math.gcd(base_w, task_w))
    width = base_w + task_w
    n_hid = width // unit_w
    n_col = d_model // COLS
    half = total // 2
    vmem = pl.BlockSpec(memory_space=pltpu.VMEM)
    hbm = pl.BlockSpec(memory_space=pl.ANY)
    dma = pltpu.SemaphoreType.DMA
    return pl.pallas_call(
        functools.partial(kernel, n_task, n_unit),
        out_shape=jax.ShapeDtypeStruct((rows, d_model), BF16),
        in_specs=[vmem, vmem] + [hbm] * 6,
        out_specs=vmem,
        scratch_shapes=[
            pltpu.VMEM((width, d_model), BF16),
            pltpu.VMEM((width, d_model), BF16),
            pltpu.VMEM((n_col - REUSE, width, COLS), BF16),
            pltpu.VMEM((n_hid, total, unit_w), BF16),
            pltpu.VMEM((total, d_model), BF16),
            pltpu.VMEM((2, n_xy, 2 * group, d_model // 2), BF16),
            pltpu.VMEM((n_task, rows, d_model), BF16),
            pltpu.VMEM((group, d_model), F32),
            pltpu.VMEM((n_unit, 1, group), F32),
            pltpu.VMEM((total, 128), F32),
            pltpu.VMEM((n_col, 2, n_xy, group, COLS), F32),
            pltpu.VMEM((n_col, half, COLS), BF16),
            pltpu.VMEM((n_col, half, COLS), BF16),
            pltpu.VMEM((n_col, n_xy, 2 * group, COLS // 2), BF16),
            pltpu.VMEM((n_col, n_xy, 2 * group, COLS // 2), BF16),
            pltpu.VMEM((n_col, n_task, rows, COLS), BF16),
            pltpu.VMEM((n_col, n_task, rows, COLS), BF16),
            pltpu.VMEM((n_col, n_task, rows, COLS), F32),
            dma((n_hid,)), dma((n_hid,)), dma((n_col, 2)),
            dma((n_task,)), dma((n_task,)),
            dma((n_xy,)), dma((n_xy,)), dma((n_xy,)), dma((n_xy,)),
            dma((n_unit,)), dma((n_unit,)),
            dma((n_col,)), dma((n_col,)),
            dma((n_col, n_xy)), dma((n_col, n_xy)),
            dma((n_col, n_task)), dma((n_col, n_task)),
        ],
        compiler_params=pltpu.CompilerParams(
            collective_id=0, has_side_effects=True, vmem_limit_bytes=VMEM_LIMIT
        ),
        cost_estimate=pl.CostEstimate(
            flops=6 * total * width * d_model,
            bytes_accessed=6 * width * d_model,
            transcendentals=total * width,
        ),
        name="router_mixture",
    )(tokens, router.reshape(1, group), bg, bu, bd, tg, tu, td)


VMEM_LIMIT = 64 * 1024 * 1024


def solution(mesh):
    in_specs = (
        P(("task", "unit"), None),
        P("unit", "task"),
        P(("task", "unit"), None),
        P(("task", "unit"), None),
        P(("task", "unit"), None),
        P("task", "unit", None),
        P("task", "unit", None),
        P("task", "unit", None),
    )
    out_specs = P(("task", "unit"), None)
    part_fn = functools.partial(body, mesh.shape["task"], mesh.shape["unit"])
    return jax.shard_map(part_fn, mesh=mesh, in_specs=in_specs, out_specs=out_specs, check_vma=False)
```

```python
import functools
import math

import jax
import jax.numpy as jnp
from jax import lax
from jax.experimental import pallas as pl
from jax.experimental.pallas import tpu as pltpu
from jax.sharding import PartitionSpec as P

MESH = pl.DeviceIdType.MESH
F32 = jnp.float32
BF16 = jnp.bfloat16
COLS = 1024
LAG = 4
REUSE = 1


def kernel(
    n_task, n_unit, tok_ref, router_ref, bg, bu, bd, tg, tu, td, out_ref,
    gate_v, up_v, down_v, hid, x_v, tokbuf, g1, rows8, wbuf, wcol,
    part, send_a, recv_a, send_b, recv_b, send_c, recv_c, own_c,
    gsem, usem, dsem, g1s, g1r, g2s, g2r, g3s, g3r, ws, wr,
    as_, ar, bs, br, cs, cr,
):
    t = lax.axis_index("task")
    u = lax.axis_index("unit")
    n_xy = n_unit // 2
    c = lax.rem(u, 2)
    xy = u // 2
    rows, d_model = tok_ref.shape
    group = n_task * rows
    tokens = group * n_unit
    half = tokens // 2
    base_w, task_w = bg.shape[0], tg.shape[1]
    n_hid, _, unit_w = hid.shape
    n_base = base_w // unit_w
    n_col = d_model // COLS
    kept = n_col - REUSE

    barrier = pltpu.get_barrier_semaphore()
    for d in range(1, n_task):
        pl.semaphore_signal(barrier, inc=1, device_id=(lax.rem(t + d, n_task), u), device_id_type=MESH)
    for d in range(1, n_unit):
        pl.semaphore_signal(barrier, inc=1, device_id=(t, lax.rem(u + d, n_unit)), device_id_type=MESH)

    for i in range(n_hid):
        for base, task, buf, sem in ((bg, tg, gate_v, gsem), (bu, tu, up_v, usem)):
            if i < n_base:
                src = base.at[pl.ds(i * unit_w, unit_w)]
            else:
                src = task.at[0, pl.ds((i - n_base) * unit_w, unit_w)]
            pltpu.make_async_copy(src, buf.at[pl.ds(i * unit_w, unit_w)], sem.at[i]).start()

    def down_copies(j):
        cols = pl.ds(j * COLS, COLS)
        if j < kept:
            lo, hi = down_v.at[j, pl.ds(0, base_w)], down_v.at[j, pl.ds(base_w, task_w)]
        else:
            spot = pl.ds((j - kept) * COLS, COLS)
            lo, hi = gate_v.at[pl.ds(0, base_w), spot], gate_v.at[pl.ds(base_w, task_w), spot]
        return (
            pltpu.make_async_copy(bd.at[:, cols], lo, dsem.at[j, 0]),
            pltpu.make_async_copy(td.at[0, :, cols], hi, dsem.at[j, 1]),
        )

    pl.semaphore_wait(barrier, n_task + n_unit - 2)

    def remote(src, dst, ssem, rsem, dev):
        return pltpu.make_async_remote_copy(
            src_ref=src, dst_ref=dst, send_sem=ssem, recv_sem=rsem, device_id=dev, device_id_type=MESH
        )

    sibling = (t, xy * 2 + 1 - c)

    def peer_xy(d):
        return lax.rem(xy + d, n_xy)

    first = [
        remote(tok_ref, g1.at[t], g1s.at[d], g1r.at[d], (lax.rem(t + d, n_task), u))
        for d in range(1, n_task)
    ]
    for copy in first:
        copy.start()
    weights = [
        remote(router_ref, wbuf.at[u], ws.at[d], wr.at[d], (t, lax.rem(u + d, n_unit)))
        for d in range(1, n_unit)
    ]
    for copy in weights:
        copy.start()
    g1[t] = tok_ref[...]
    wbuf[u] = router_ref[...]
    for copy in first:
        copy.wait()
    for s in range(n_task):
        rows8[pl.ds(s * rows, rows), :] = g1[s].astype(F32)
    whole = rows8[...]
    mid = d_model // 2
    tokbuf[c, xy] = jnp.concatenate([whole[:, :mid], whole[:, mid:]], 0).astype(BF16)
    second = [
        remote(tokbuf.at[c, xy], tokbuf.at[c, xy], g2s.at[d], g2r.at[d], (t, peer_xy(d) * 2 + c))
        for d in range(1, n_xy)
    ]
    for copy in second:
        copy.start()
    third = [remote(tokbuf.at[c, xy], tokbuf.at[c, xy], g3s.at[0], g3r.at[0], sibling)]
    third[0].start()
    for d in range(1, n_xy):
        came = lax.rem(xy + n_xy - d, n_xy)
        remote(tokbuf.at[c, came], tokbuf.at[c, came], g2s.at[d], g2r.at[d], sibling).wait_recv()
        third.append(remote(tokbuf.at[c, came], tokbuf.at[c, came], g3s.at[d], g3r.at[d], sibling))
        third[-1].start()

    for j in range(kept):
        for copy in down_copies(j):
            copy.start()

    for copy in weights:
        copy.wait()
    shape = (tokens, group)
    place = lax.broadcasted_iota(jnp.int32, shape, 0)
    lane = lax.broadcasted_iota(jnp.int32, shape, 1)
    block = place // group
    unit_of = lax.rem(block, n_xy) * 2 + block // n_xy
    inner = lax.rem(place, group)
    token = ((inner // rows) * n_unit + unit_of) * rows + lax.rem(inner, rows)
    picked = jnp.zeros(shape, F32)
    for s in range(n_unit):
        picked = picked + jnp.where(token == lane + s * group, wbuf[s], 0.0)
    wcol[...] = jnp.broadcast_to(jnp.sum(picked, 1, keepdims=True), wcol.shape)

    for copy in second:
        copy.wait_send()
    for copy in third:
        copy.wait()
    for core in range(2):
        for p in range(0, n_xy, 2):
            parts = []
            for q in (p, p + 1):
                both = tokbuf[core, q].astype(F32)
                parts.append(jnp.concatenate([both[:group], both[group:]], 1))
            x_v[pl.ds((core * n_xy + p) * group, 2 * group), :] = jnp.concatenate(parts, 0).astype(BF16)

    dims = (((1,), (1,)), ((), ()))

    def hidden(i, _):
        spot = pl.ds(pl.multiple_of(i * unit_w, unit_w), unit_w)
        pltpu.make_async_copy(tg.at[0, pl.ds(0, unit_w)], gate_v.at[spot], gsem.at[i]).wait()
        pltpu.make_async_copy(tu.at[0, pl.ds(0, unit_w)], up_v.at[spot], usem.at[i]).wait()
        x = x_v[...]
        g = lax.dot_general(x, gate_v[spot, :], dims, preferred_element_type=F32)
        v = lax.dot_general(x, up_v[spot, :], dims, preferred_element_type=F32)
        scale = jnp.where(i < n_base, 1.0, wcol[:, :1])
        hid[i] = (jax.nn.silu(g) * v * scale).astype(BF16)
        return 0

    lax.fori_loop(0, n_hid, hidden, 0)

    for j in range(kept, n_col):
        for copy in down_copies(j):
            copy.start()

    pending = []

    def stage_a(j):
        for copy in down_copies(j):
            copy.wait()
        weight = down_v.at[j] if j < kept else gate_v.at[:, pl.ds((j - kept) * COLS, COLS)]
        if unit_w % 128 == 0:
            h = jnp.concatenate([hid[i] for i in range(n_hid)], 1)
            total = jnp.dot(h, weight[...], preferred_element_type=F32)
        else:
            total = jnp.zeros((tokens, COLS), F32)
            for i in range(n_hid):
                total += jnp.dot(hid[i], weight[pl.ds(i * unit_w, unit_w), :], preferred_element_type=F32)
        part[j] = total.reshape(2, n_xy, group, COLS)
        send_a[j] = part[j, 1 - c].reshape(half, COLS).astype(BF16)
        copy = remote(send_a.at[j], recv_a.at[j], as_.at[j], ar.at[j], sibling)
        copy.start()
        pending.append(copy)

    def stage_b(j):
        remote(send_a.at[j], recv_a.at[j], as_.at[j], ar.at[j], sibling).wait_recv()
        part[j, c] += recv_a[j].astype(F32).reshape(n_xy, group, COLS)
        for d in range(1, n_xy):
            block = part[j, c, peer_xy(d)]
            send_b[j, d] = jnp.concatenate([block[:, : COLS // 2], block[:, COLS // 2 :]], 0).astype(BF16)
            copy = remote(send_b.at[j, d], recv_b.at[j, d], bs.at[j, d], br.at[j, d], (t, peer_xy(d) * 2 + c))
            copy.start()
            pending.append(copy)

    def stage_c(j):
        total = part[j, c, xy]
        for d in range(1, n_xy):
            remote(send_b.at[j, d], recv_b.at[j, d], bs.at[j, d], br.at[j, d], sibling).wait_recv()
            both = recv_b[j, d].astype(F32)
            total = total + jnp.concatenate([both[:group], both[group:]], 1)
        for s in range(n_task):
            piece = total[s * rows : (s + 1) * rows]
            own_c[j, s] = piece
            send_c[j, s] = piece.astype(BF16)
        for d in range(1, n_task):
            to = lax.rem(t + d, n_task)
            copy = remote(send_c.at[j, to], recv_c.at[j, d], cs.at[j, d], cr.at[j, d], (to, u))
            copy.start()
            pending.append(copy)

    def stage_d(j):
        total = own_c[j, t]
        for d in range(1, n_task):
            remote(send_c.at[j, 0], recv_c.at[j, d], cs.at[j, d], cr.at[j, d], sibling).wait_recv()
            total = total + recv_c[j, d].astype(F32)
        out_ref[:, pl.ds(j * COLS, COLS)] = total.astype(BF16)

    for step in range(n_col + 3 * LAG):
        for lag, stage in ((0, stage_a), (LAG, stage_b), (2 * LAG, stage_c), (3 * LAG, stage_d)):
            if 0 <= step - lag < n_col:
                stage(step - lag)
    for copy in pending:
        copy.wait_send()


def body(n_task, n_unit, tokens, router, bg, bu, bd, tg, tu, td):
    rows, d_model = tokens.shape
    group = n_task * rows
    total = group * n_unit
    n_xy = n_unit // 2
    base_w, task_w = bg.shape[0], tg.shape[1]
    unit_w = min(512, math.gcd(base_w, task_w))
    width = base_w + task_w
    n_hid = width // unit_w
    n_col = d_model // COLS
    half = total // 2
    vmem = pl.BlockSpec(memory_space=pltpu.VMEM)
    hbm = pl.BlockSpec(memory_space=pl.ANY)
    dma = pltpu.SemaphoreType.DMA
    return pl.pallas_call(
        functools.partial(kernel, n_task, n_unit),
        out_shape=jax.ShapeDtypeStruct((rows, d_model), BF16),
        in_specs=[vmem, vmem] + [hbm] * 6,
        out_specs=vmem,
        scratch_shapes=[
            pltpu.VMEM((width, d_model), BF16),
            pltpu.VMEM((width, d_model), BF16),
            pltpu.VMEM((n_col - REUSE, width, COLS), BF16),
            pltpu.VMEM((n_hid, total, unit_w), BF16),
            pltpu.VMEM((total, d_model), BF16),
            pltpu.VMEM((2, n_xy, 2 * group, d_model // 2), BF16),
            pltpu.VMEM((n_task, rows, d_model), BF16),
            pltpu.VMEM((group, d_model), F32),
            pltpu.VMEM((n_unit, 1, group), F32),
            pltpu.VMEM((total, 128), F32),
            pltpu.VMEM((n_col, 2, n_xy, group, COLS), F32),
            pltpu.VMEM((n_col, half, COLS), BF16),
            pltpu.VMEM((n_col, half, COLS), BF16),
            pltpu.VMEM((n_col, n_xy, 2 * group, COLS // 2), BF16),
            pltpu.VMEM((n_col, n_xy, 2 * group, COLS // 2), BF16),
            pltpu.VMEM((n_col, n_task, rows, COLS), BF16),
            pltpu.VMEM((n_col, n_task, rows, COLS), BF16),
            pltpu.VMEM((n_col, n_task, rows, COLS), F32),
            dma((n_hid,)), dma((n_hid,)), dma((n_col, 2)),
            dma((n_task,)), dma((n_task,)),
            dma((n_xy,)), dma((n_xy,)), dma((n_xy,)), dma((n_xy,)),
            dma((n_unit,)), dma((n_unit,)),
            dma((n_col,)), dma((n_col,)),
            dma((n_col, n_xy)), dma((n_col, n_xy)),
            dma((n_col, n_task)), dma((n_col, n_task)),
        ],
        compiler_params=pltpu.CompilerParams(
            collective_id=0, has_side_effects=True, vmem_limit_bytes=VMEM_LIMIT
        ),
        cost_estimate=pl.CostEstimate(
            flops=6 * total * width * d_model,
            bytes_accessed=6 * width * d_model,
            transcendentals=total * width,
        ),
        name="router_mixture",
    )(tokens, router.reshape(1, group), bg, bu, bd, tg, tu, td)


VMEM_LIMIT = 64 * 1024 * 1024


def solution(mesh):
    in_specs = (
        P(("task", "unit"), None),
        P("unit", "task"),
        P(("task", "unit"), None),
        P(("task", "unit"), None),
        P(("task", "unit"), None),
        P("task", "unit", None),
        P("task", "unit", None),
        P("task", "unit", None),
    )
    out_specs = P(("task", "unit"), None)
    part_fn = functools.partial(body, mesh.shape["task"], mesh.shape["unit"])
    return jax.shard_map(part_fn, mesh=mesh, in_specs=in_specs, out_specs=out_specs, check_vma=False)
```
